32 devices in a mesh: space: 8 (over y, x, core), tm: 4 (over z).
Axes of the slice: x: 2, y: 2, z: 4, core: 2. Of those that a mesh axis runs over, the one named last changes fastest.
Arguments:
- field: bfloat16 [114688, 1024], P('space', 'tm'), may hold values from -6 to 6
- sp_blocks: bfloat16 [896, 5, 128, 128], P('space'), may hold values from -0.25 to 0.25
- sp_cols: int32 [896, 5], P('space'), may hold values from 0 to 895, as said below
- sp_count: int32 [896], P('space'), may hold values from 1 to 5, as said below
- tm_factor: bfloat16 [1024, 1024], replicated, may hold values from -0.1875 to 0.1875
Outputs:
- scores: float32 [114688], P(('space', 'tm'))
The draws below stay inside these ranges and needn't reach their ends.
Inputs may be any that keep to these rules, and one draw needn't show every extreme that they name: `sp_count`: live slots come first; some row block has 5 live slots. `sp_cols`: slot 0 of row block r names r. Live slots 1 and on name distinct blocks (r + d) mod 896 with 1 <= |d| <= 112. Slots that are not live name r.
All inputs are finite; a program needn't handle non-finite values.
Results may differ from the reference program's by a relative error of at most 0.00038.
Values may be sent and summed in bfloat16 or wider, within the bound.
A program may use at most 192 MiB of HBM per device.

```python
import jax
import jax.numpy as jnp
from jax import lax

STEPS = 1024
BLOCK = 128
SLOTS = 5
BLOCKS_DEV = 112
NODE_BLOCKS = 896
NODES = 114688


def pattern_draw(key):
    base_key = jax.random.fold_in(key, 7)
    key_list = jax.random.split(base_key, 5)
    device_count = NODE_BLOCKS // BLOCKS_DEV
    cap_limit = jax.random.randint(key_list[0], (device_count,), 2, SLOTS + 1)
    fullest = jax.random.randint(key_list[1], (), 0, device_count)
    cap_limit = jnp.where(jnp.arange(device_count) == fullest, SLOTS, cap_limit)
    counts = jax.random.randint(key_list[2], (device_count, BLOCKS_DEV), 1, cap_limit[:, None] + 1)
    chosen = jax.random.randint(key_list[3], (device_count,), 0, BLOCKS_DEV)
    counts = jnp.where(jnp.arange(BLOCKS_DEV)[None, :] == chosen[:, None], cap_limit[:, None], counts)
    counts = counts.reshape(NODE_BLOCKS)
    reach_span = 2 * BLOCKS_DEV
    rank_value = jax.random.randint(key_list[4], (NODE_BLOCKS, reach_span), 0, 1 << 20) * reach_span + jnp.arange(reach_span)[None, :]
    chosen_rank = jnp.argsort(rank_value, axis=1)[:, :SLOTS - 1]
    shift_by = jnp.where(chosen_rank < BLOCKS_DEV, chosen_rank - BLOCKS_DEV, chosen_rank - BLOCKS_DEV + 1)
    row_index = jnp.arange(NODE_BLOCKS)[:, None]
    far_cols = jnp.mod(row_index + shift_by, NODE_BLOCKS)
    col_index = jnp.concatenate([row_index, far_cols], axis=1)
    slot_index = jnp.arange(SLOTS)[None, :]
    col_index = jnp.where(slot_index < counts[:, None], col_index, row_index)
    return (counts.astype(jnp.int32), col_index.astype(jnp.int32))


def draw_sp_count(key, part):
    return pattern_draw(key)[0]


def draw_sp_cols(key, part):
    return pattern_draw(key)[1]


def block_scale(stream_key, shape, cuts, smallest, top_value):
    loudness, own = 1.0, jax.random.fold_in(stream_key, 6)
    for position, blocks in cuts:
        heights = jnp.exp(jax.random.uniform(jax.random.fold_in(own, position), (blocks,), jnp.float32, smallest / len(cuts), top_value / len(cuts)))
        loudness = loudness * jnp.repeat(heights, shape[position] // blocks).reshape([-1 if axis == position else 1 for axis in range(len(shape))])
    return loudness


def noise(stream_key, dims, spread, bound, cuts=(), kind=jnp.bfloat16):
    array = jax.random.normal(stream_key, dims, jnp.float32) * spread
    if len(cuts) > 0:
        array = block_scale(stream_key, dims, cuts, -0.22, 0.18) * array
    return jnp.clip(array, min=-bound, max=bound).astype(kind)


def setup_inputs(seed: int = 0) -> dict:
    streams_of = jax.random.split(jax.random.key(seed), 6)
    field = noise(streams_of[0], (NODES, STEPS), 1.0, 6.0, ((0, 8), (1, 4)))
    sp_blocks = noise(streams_of[1], (NODE_BLOCKS, SLOTS, BLOCK, BLOCK), (BLOCK * SLOTS) ** -0.5, 0.25, ((0, 8),))
    sp_cols = draw_sp_cols(jax.random.fold_in(streams_of[5], 71), 0)
    sp_count = draw_sp_count(jax.random.fold_in(streams_of[5], 71), 0)
    tm_factor = noise(streams_of[4], (STEPS, STEPS), STEPS ** -0.5, 0.1875)
    return dict(field=field, sp_blocks=sp_blocks, sp_cols=sp_cols, sp_count=sp_count, tm_factor=tm_factor)


def reference(field, sp_blocks, sp_cols, sp_count, tm_factor):
    node_blocks = field.reshape(NODE_BLOCKS, BLOCK, STEPS)
    alive_mask = jnp.arange(SLOTS, dtype=jnp.int32)[None, :] < sp_count[:, None]
    group_count = NODE_BLOCKS // BLOCKS_DEV

    def group_score(group_args):
        blocks, col_index, alive_slot = group_args
        picked = node_blocks[col_index].astype(jnp.float32)
        weights = jnp.where(alive_slot[:, :, None, None], blocks.astype(jnp.float32), 0.0)
        spatial = jnp.einsum("gkab,gkbt->gat", weights, picked).astype(jnp.bfloat16)
        whitened = jnp.dot(spatial.reshape(BLOCKS_DEV * BLOCK, STEPS), tm_factor, preferred_element_type=jnp.float32)
        return jnp.sum(whitened * whitened, axis=1) / STEPS

    scores = lax.map(group_score, (sp_blocks.reshape(group_count, BLOCKS_DEV, SLOTS, BLOCK, BLOCK),
                                   sp_cols.reshape(group_count, BLOCKS_DEV, SLOTS),
                                   alive_mask.reshape(group_count, BLOCKS_DEV, SLOTS)))
    return scores.reshape(NODES)
```

```python
import functools

import jax
import jax.numpy as jnp
from jax import lax
from jax.experimental import pallas as pl
from jax.experimental.pallas import tpu as pltpu
from jax.sharding import PartitionSpec as P

LANES = 128


def spatial_kernel(group, slots, block, pos_ref, blocks_ref, left_ref, own_ref, right_ref, out_ref, near, sems):
    nodes = own_ref.shape[0]
    step = pl.program_id(0)

    @pl.when(step == 0)
    def _():
        parts = (left_ref, own_ref, right_ref)
        copies = [
            pltpu.make_async_copy(part, near.at[pl.ds(i * nodes, nodes)], sems.at[i])
            for i, part in enumerate(parts)
        ]
        for copy in copies:
            copy.start()
        near[pl.ds(3 * nodes, block), :] = jnp.zeros((block, near.shape[1]), near.dtype)
        for copy in copies:
            copy.wait()

    for i in range(group):
        row = step * group + i
        weights = jnp.concatenate([blocks_ref[i, k] for k in range(slots)], axis=1)
        picked = jnp.concatenate(
            [near[pl.ds(pl.multiple_of(pos_ref[row * slots + k] * block, block), block), :] for k in range(slots)],
            axis=0,
        )
        out_ref[pl.ds(i * block, block), :] = jnp.dot(
            weights, picked, preferred_element_type=jnp.float32
        ).astype(out_ref.dtype)


def spatial_of(position, sp_blocks, left, own, right):
    blocks_dev, slots, block, _ = sp_blocks.shape
    nodes, width = own.shape
    group = 8
    any_spec = pl.BlockSpec(memory_space=pl.ANY)
    return pl.pallas_call(
        functools.partial(spatial_kernel, group, slots, block),
        out_shape=jax.ShapeDtypeStruct((nodes, width), jnp.bfloat16),
        grid_spec=pltpu.PrefetchScalarGridSpec(
            num_scalar_prefetch=1,
            grid=(blocks_dev // group,),
            in_specs=[
                pl.BlockSpec((group, slots, block, block), lambda g, *_: (g, 0, 0, 0)),
                any_spec,
                any_spec,
                any_spec,
            ],
            out_specs=pl.BlockSpec((group * block, width), lambda g, *_: (g, 0)),
            scratch_shapes=[
                pltpu.VMEM((3 * nodes + block, width), jnp.bfloat16),
                pltpu.SemaphoreType.DMA((3,)),
            ],
        ),
        compiler_params=pltpu.CompilerParams(vmem_limit_bytes=32 << 20),
        cost_estimate=pl.CostEstimate(
            flops=2 * nodes * block * slots * width,
            bytes_accessed=2 * sp_blocks.size + 8 * nodes * width,
            transcendentals=0,
        ),
    )(position, sp_blocks, left, own, right)


def score_kernel(sources, chunks, slab, src_ref, factor_ref, *refs):
    pieces, out_ref = refs[:-1], refs[-1]
    steps = factor_ref.shape[0]
    tile = pieces[0].shape[0]
    total = None
    for s in range(sources):
        cells = jnp.concatenate([pieces[s * chunks + c][...] for c in range(chunks)], axis=1)
        rows = factor_ref[pl.ds(pl.multiple_of(src_ref[s] * slab, slab), slab), :]
        part = jnp.dot(cells, rows, preferred_element_type=jnp.float32)
        total = part if total is None else total + part
    square = total * total
    folded = square[:, :LANES]
    for c in range(1, steps // LANES):
        folded = folded + square[:, c * LANES : (c + 1) * LANES]
    for j in range(tile // LANES):
        column = jnp.sum(folded[j * LANES : (j + 1) * LANES, :].T, axis=0, keepdims=True)
        out_ref[pl.ds(pl.program_id(0) * (tile // LANES) + j, 1), :] = column / steps


def scores_of(src, tm_factor, pieces, slab):
    rows, width = pieces[0].shape
    chunks = slab // width
    steps = tm_factor.shape[0]
    tile = 256
    out = pl.pallas_call(
        functools.partial(score_kernel, len(pieces) // chunks, chunks, slab),
        out_shape=jax.ShapeDtypeStruct((rows // LANES, LANES), jnp.float32),
        grid_spec=pltpu.PrefetchScalarGridSpec(
            num_scalar_prefetch=1,
            grid=(rows // tile,),
            in_specs=[pl.BlockSpec((steps, steps), lambda g, *_: (0, 0))]
            + [pl.BlockSpec((tile, width), lambda g, *_: (g, 0))] * len(pieces),
            out_specs=pl.BlockSpec((rows // LANES, LANES), lambda g, *_: (0, 0)),
        ),
        compiler_params=pltpu.CompilerParams(vmem_limit_bytes=32 << 20),
        cost_estimate=pl.CostEstimate(
            flops=2 * rows * steps * steps, bytes_accessed=2 * rows * steps + 2 * steps * steps, transcendentals=0
        ),
    )(src, tm_factor, *pieces)
    return out.reshape(rows)


def on_device(field, sp_blocks, sp_cols, sp_count, tm_factor):
    blocks_dev, slots = sp_cols.shape
    slab = field.shape[1]
    space_count, tm_count = lax.axis_size("space"), lax.axis_size("tm")
    total_blocks = blocks_dev * space_count
    local = jnp.arange(blocks_dev, dtype=jnp.int32)[:, None]
    row_index = lax.axis_index("space") * blocks_dev + local
    position = local + jnp.mod(sp_cols - row_index + blocks_dev, total_blocks)
    alive = jnp.arange(slots, dtype=jnp.int32)[None, :] < sp_count[:, None]
    position = jnp.where(alive, position, 3 * blocks_dev).reshape(-1)

    up = [(i, (i + 1) % space_count) for i in range(space_count)]
    down = [((i + 1) % space_count, i) for i in range(space_count)]
    me = lax.axis_index("tm")
    rows = field.shape[0] // tm_count
    chunks = slab // LANES
    received = [[None] * chunks for _ in range(tm_count)]
    left = right = None
    for c in range(chunks):
        own = lax.slice_in_dim(field, c * LANES, (c + 1) * LANES, axis=1)
        if left is not None:
            own, left, right = lax.optimization_barrier((own, left, right))
        new_left = lax.ppermute(own, "space", up)
        new_right = lax.ppermute(own, "space", down)
        left, right = new_left, new_right
        spatial = spatial_of(position, sp_blocks, left, own, right)
        for k in range(tm_count):
            target = lax.rem(me + k, tm_count)
            piece = lax.dynamic_slice_in_dim(spatial, target * rows, rows, 0)
            if k:
                piece = lax.ppermute(piece, "tm", [(i, (i + k) % tm_count) for i in range(tm_count)])
            received[k][c] = piece
    src = jnp.stack([lax.rem(me - k + tm_count, tm_count) for k in range(tm_count)]).astype(jnp.int32)
    return scores_of(src, tm_factor, [p for group in received for p in group], slab)


def solution(mesh):
    in_specs = (P("space", "tm"), P("space", None, None, None), P("space", None), P("space"), P())
    out_specs = P(("space", "tm"))
    return jax.shard_map(
        on_device, mesh=mesh, in_specs=in_specs, out_specs=out_specs, check_vma=False
    )
```

```python
import functools

import jax
import jax.numpy as jnp
from jax import lax
from jax.experimental import pallas as pl
from jax.experimental.pallas import tpu as pltpu
from jax.sharding import PartitionSpec as P

LANES = 128
PIECES = 8
AHEAD = 3
MESH = pl.DeviceIdType.MESH


def kernel(dims, field_ref, blocks_ref, pos_ref, factor_ref, out_ref, *scratch):
    blocks_dev, slots, block, chunks, space_count, tm_count = dims
    near = scratch[:chunks]
    (land, blocks_buf, spatial, received, factor,
     own_sems, fast_send, fast_recv, slow_send, slow_recv,
     blocks_sems, z_send, z_recv, local_sem, factor_sem) = scratch[chunks:]
    piece_blocks = blocks_dev // PIECES
    piece = piece_blocks * block
    steps_all = chunks * PIECES
    per_tm = PIECES // tm_count
    slab = chunks * LANES

    place = lax.axis_index("space")
    me = lax.axis_index("tm")
    odd = lax.rem(place, 2)
    sibling = place + 1 - 2 * odd
    far = lax.rem(place + 2 * odd - 1 + space_count, space_count)

    def ordered(g, first_up, count):
        return first_up * g + (1 - first_up) * (count - 1 - g)

    barrier = pltpu.get_barrier_semaphore()
    for other in (sibling, far):
        pl.semaphore_signal(barrier, inc=1, device_id=(other, me), device_id_type=MESH)
    for k in range(1, tm_count):
        pl.semaphore_signal(
            barrier, inc=1, device_id=(place, lax.rem(me + k, tm_count)), device_id_type=MESH
        )
    pl.semaphore_wait(barrier, tm_count + 1)

    def slow_copy(n):
        g, c = lax.rem(n, PIECES), n // PIECES
        start = ordered(g, 1 - odd, PIECES) * piece_blocks
        return pltpu.make_async_remote_copy(
            src_ref=field_ref.at[pl.ds(start, piece_blocks), :, pl.ds(pl.multiple_of(c * LANES, LANES), LANES)],
            dst_ref=land.at[n],
            send_sem=slow_send.at[n],
            recv_sem=slow_recv.at[n],
            device_id=(far, me),
            device_id_type=MESH,
        )

    def fast_copy(c):
        return pltpu.make_async_remote_copy(
            src_ref=field_ref.at[:, :, pl.ds(c * LANES, LANES)],
            dst_ref=near[c].at[pl.ds(odd * (2 * blocks_dev), blocks_dev)],
            send_sem=fast_send.at[c],
            recv_sem=fast_recv.at[c],
            device_id=(sibling, me),
            device_id_type=MESH,
        )

    def own_copy(c):
        return pltpu.make_async_copy(
            field_ref.at[:, :, pl.ds(c * LANES, LANES)], near[c].at[pl.ds(blocks_dev, blocks_dev)], own_sems.at[c]
        )

    def blocks_copy(n):
        start = ordered(lax.rem(n, PIECES), odd, PIECES) * piece_blocks
        slot = lax.rem(n, 2)
        return pltpu.make_async_copy(
            blocks_ref.at[pl.ds(start, piece_blocks)], blocks_buf.at[slot], blocks_sems.at[slot]
        )

    def target_of(g):
        p = ordered(g, odd, PIECES)
        return p, p // per_tm, lax.rem(p, per_tm)

    def z_copy(c, g):
        p, target, half = target_of(g)
        return pltpu.make_async_remote_copy(
            src_ref=spatial.at[c * PIECES + p],
            dst_ref=received.at[(me * chunks + c) * per_tm + half],
            send_sem=z_send.at[c * PIECES + g],
            recv_sem=z_recv.at[(me * chunks + c) * per_tm + half],
            device_id=(place, target),
            device_id_type=MESH,
        )

    slow_copy(0).start()
    fast_copy(0).start()
    for n in range(1, AHEAD):
        slow_copy(n).start()
    for c in range(chunks):
        own_copy(c).start()
    blocks_copy(0).start()
    factor_copy = pltpu.make_async_copy(factor_ref, factor, factor_sem)
    factor_copy.start()
    for c in range(chunks):
        near[c][3 * blocks_dev] = jnp.zeros((block, LANES), jnp.bfloat16)

    for c in range(chunks):
        own_copy(c).wait()
        fast_copy(c).wait()
        if c + 1 < chunks:
            fast_copy(c + 1).start()

        def stage(g, carry):
            n = c * PIECES + g
            p, target, half = target_of(g)

            @pl.when(n + 1 < steps_all)
            def _():
                blocks_copy(n + 1).start()

            arriving = slow_copy(n)
            arriving.wait_recv()
            arriving.wait_send()

            @pl.when(n + AHEAD < steps_all)
            def _():
                slow_copy(n + AHEAD).start()

            near[c][pl.ds(odd * (2 * blocks_dev) + p * piece_blocks, piece_blocks)] = land[n]
            blocks_copy(n).wait()
            slot = lax.rem(n, 2)

            def row(i, carry):
                base = (p * piece_blocks + i) * slots
                weights = jnp.concatenate([blocks_buf[slot, i, k] for k in range(slots)], axis=1)
                picked = jnp.concatenate(
                    [near[c][pos_ref[base + k]] for k in range(slots)], axis=0
                )
                spatial[c * PIECES + p, pl.ds(pl.multiple_of(i * block, block), block), :] = jnp.dot(
                    weights, picked, preferred_element_type=jnp.float32
                ).astype(jnp.bfloat16)
                return carry

            lax.fori_loop(0, piece_blocks, row, 0, unroll=2)

            @pl.when(target != me)
            def _():
                z_copy(c, g).start()

            @pl.when(target == me)
            def _():
                keep = pltpu.make_async_copy(
                    spatial.at[c * PIECES + p], received.at[(me * chunks + c) * per_tm + half], local_sem
                )
                keep.start()
                keep.wait()

            return carry

        lax.fori_loop(0, PIECES, stage, 0)

    factor_copy.wait()
    tile = 256
    width = factor.shape[0]
    for k in range(per_tm):
        half = ordered(k, odd, per_tm)
        for s in range(tm_count):

            @pl.when(me != s)
            def _():
                for c in range(chunks):
                    slot = (s * chunks + c) * per_tm + half
                    pltpu.make_async_remote_copy(
                        src_ref=received.at[slot],
                        dst_ref=received.at[slot],
                        send_sem=z_send.at[0],
                        recv_sem=z_recv.at[slot],
                        device_id=(place, s),
                        device_id_type=MESH,
                    ).wait_recv()

        def score(t, carry):
            rows = pl.ds(pl.multiple_of(t * tile, tile), tile)
            total = None
            for s in range(tm_count):
                cells = jnp.concatenate(
                    [received[(s * chunks + c) * per_tm + half, rows, :] for c in range(chunks)], axis=1
                )
                part = jnp.dot(cells, factor[s * slab : (s + 1) * slab, :], preferred_element_type=jnp.float32)
                total = part if total is None else total + part
            square = total * total
            folded = square[:, :LANES]
            for c in range(1, width // LANES):
                folded = folded + square[:, c * LANES : (c + 1) * LANES]
            for j in range(tile // LANES):
                column = jnp.sum(folded[j * LANES : (j + 1) * LANES, :].T, axis=0, keepdims=True)
                out_ref[pl.ds(half * (piece // LANES) + t * (tile // LANES) + j, 1), :] = column / width
            return carry

        lax.fori_loop(0, piece // tile, score, 0)

    for c in range(chunks):

        def finish(g, carry):
            _, target, _ = target_of(g)

            @pl.when(target != me)
            def _():
                z_copy(c, g).wait_send()

            return carry

        lax.fori_loop(0, PIECES, finish, 0)


def on_device(field, sp_blocks, sp_cols, sp_count, tm_factor):
    blocks_dev, slots, block, _ = sp_blocks.shape
    nodes, slab = field.shape
    space_count, tm_count = lax.axis_size("space"), lax.axis_size("tm")
    total_blocks = blocks_dev * space_count
    chunks = slab // LANES
    local = jnp.arange(blocks_dev, dtype=jnp.int32)[:, None]
    row_index = lax.axis_index("space") * blocks_dev + local
    position = local + jnp.mod(sp_cols - row_index + blocks_dev, total_blocks)
    alive = jnp.arange(slots, dtype=jnp.int32)[None, :] < sp_count[:, None]
    position = jnp.where(alive, position, 3 * blocks_dev).reshape(-1)

    piece = nodes // PIECES
    rows = nodes // tm_count
    per_tm = PIECES // tm_count
    steps_all = chunks * PIECES
    any_spec = pl.BlockSpec(memory_space=pl.ANY)
    dma = pltpu.SemaphoreType.DMA
    out = pl.pallas_call(
        functools.partial(kernel, (blocks_dev, slots, block, chunks, space_count, tm_count)),
        out_shape=jax.ShapeDtypeStruct((rows // LANES, LANES), jnp.float32),
        in_specs=[any_spec, any_spec, pl.BlockSpec(memory_space=pltpu.SMEM), any_spec],
        out_specs=pl.BlockSpec(memory_space=pltpu.VMEM),
        scratch_shapes=[pltpu.VMEM((3 * blocks_dev + 1, block, LANES), jnp.bfloat16) for _ in range(chunks)]
        + [
            pltpu.VMEM((steps_all, piece // block, block, LANES), jnp.bfloat16),
            pltpu.VMEM((2, blocks_dev // PIECES, slots, block, block), jnp.bfloat16),
            pltpu.VMEM((steps_all, piece, LANES), jnp.bfloat16),
            pltpu.VMEM((tm_count * chunks * per_tm, piece, LANES), jnp.bfloat16),
            pltpu.VMEM(tm_factor.shape, jnp.bfloat16),
            dma((chunks,)),
            dma((chunks,)),
            dma((chunks,)),
            dma((steps_all,)),
            dma((steps_all,)),
            dma((2,)),
            dma((steps_all,)),
            dma((tm_count * chunks * per_tm,)),
            dma,
            dma,
        ],
        compiler_params=pltpu.CompilerParams(
            collective_id=0, has_side_effects=True, vmem_limit_bytes=58 << 20
        ),
        cost_estimate=pl.CostEstimate(
            flops=2 * nodes * slab * (block * slots + tm_factor.shape[1]),
            bytes_accessed=2 * sp_blocks.size * chunks + 4 * field.size + 2 * tm_factor.size,
            transcendentals=0,
        ),
    )(field.reshape(blocks_dev, block, slab), sp_blocks, position, tm_factor)
    return out.reshape(rows)


def solution(mesh):
    in_specs = (P("space", "tm"), P("space", None, None, None), P("space", None), P("space"), P())
    out_specs = P(("space", "tm"))
    return jax.shard_map(
        on_device, mesh=mesh, in_specs=in_specs, out_specs=out_specs, check_vma=False
    )
```

```python
import functools

import jax
import jax.numpy as jnp
from jax import lax
from jax.experimental import pallas as pl
from jax.experimental.pallas import tpu as pltpu
from jax.sharding import PartitionSpec as P

LANES = 128
PIECES = 14
AHEAD = 4
LAG = 3
MESH = pl.DeviceIdType.MESH


def kernel(dims, field_ref, blocks_ref, pos_ref, factor_ref, out_ref, *scratch):
    blocks_dev, slots, block, chunks, space_count, tm_count = dims
    near = scratch[:chunks]
    (land, blocks_buf, spatial, received, factor,
     own_sems, fast_send, fast_recv, slow_send, slow_recv,
     blocks_sems, z_send, z_recv, factor_sem, shared, share_send, share_recv) = scratch[chunks:]
    piece_blocks = blocks_dev // PIECES
    steps_all = chunks * PIECES
    part = piece_blocks // tm_count
    slab = chunks * LANES

    place = lax.axis_index("space")
    me = lax.axis_index("tm")
    odd = lax.rem(place, 2)
    sibling = place + 1 - 2 * odd
    far = lax.rem(place + 2 * odd - 1 + space_count, space_count)

    def ordered(g, first_up, count):
        return first_up * g + (1 - first_up) * (count - 1 - g)

    barrier = pltpu.get_barrier_semaphore()
    for other in (sibling, far):
        pl.semaphore_signal(barrier, inc=1, device_id=(other, me), device_id_type=MESH)
    for k in range(1, tm_count):
        pl.semaphore_signal(
            barrier, inc=1, device_id=(place, lax.rem(me + k, tm_count)), device_id_type=MESH
        )
    pl.semaphore_wait(barrier, tm_count + 1)

    def slow_copy(n):
        g, c = lax.rem(n, PIECES), n // PIECES
        start = ordered(g, 1 - odd, PIECES) * piece_blocks
        return pltpu.make_async_remote_copy(
            src_ref=field_ref.at[pl.ds(start, piece_blocks), :, pl.ds(pl.multiple_of(c * LANES, LANES), LANES)],
            dst_ref=land.at[n],
            send_sem=slow_send.at[n],
            recv_sem=slow_recv.at[n],
            device_id=(far, me),
            device_id_type=MESH,
        )

    def fast_copy(c):
        return pltpu.make_async_remote_copy(
            src_ref=field_ref.at[:, :, pl.ds(c * LANES, LANES)],
            dst_ref=near[c].at[pl.ds(odd * (2 * blocks_dev), blocks_dev)],
            send_sem=fast_send.at[c],
            recv_sem=fast_recv.at[c],
            device_id=(sibling, me),
            device_id_type=MESH,
        )

    def own_copy(c):
        return pltpu.make_async_copy(
            field_ref.at[:, :, pl.ds(c * LANES, LANES)], near[c].at[pl.ds(blocks_dev, blocks_dev)], own_sems.at[c]
        )

    def blocks_copy(n):
        start = ordered(lax.rem(n, PIECES), odd, PIECES) * piece_blocks
        slot = lax.rem(n, 2)
        return pltpu.make_async_copy(
            blocks_ref.at[pl.ds(start, piece_blocks)], blocks_buf.at[slot], blocks_sems.at[slot]
        )

    def place_of(source, c, p):
        return (source * chunks + c) * PIECES + p

    def z_copy(c, g, k):
        p, target = ordered(g, odd, PIECES), lax.rem(me + k, tm_count)
        return pltpu.make_async_remote_copy(
            src_ref=spatial.at[c * PIECES + p, pl.ds(target * part, part)],
            dst_ref=received.at[place_of(me, c, p)],
            send_sem=z_send.at[(c * PIECES + g) * (tm_count - 1) + k - 1],
            recv_sem=z_recv.at[place_of(me, c, p)],
            device_id=(place, target),
            device_id_type=MESH,
        )

    def z_arrival(c, g, k):
        p, source = ordered(g, odd, PIECES), lax.rem(me + k, tm_count)
        here = received.at[place_of(source, c, p)]
        return pltpu.make_async_remote_copy(
            src_ref=here,
            dst_ref=here,
            send_sem=z_send.at[0],
            recv_sem=z_recv.at[place_of(source, c, p)],
            device_id=(place, source),
            device_id_type=MESH,
        )

    def share_copy(k):
        return pltpu.make_async_remote_copy(
            src_ref=shared.at[me],
            dst_ref=shared.at[me],
            send_sem=share_send.at[k - 1],
            recv_sem=share_recv.at[me],
            device_id=(place, lax.rem(me + k, tm_count)),
            device_id_type=MESH,
        )

    def share_arrival(k):
        source = lax.rem(me + k, tm_count)
        return pltpu.make_async_remote_copy(
            src_ref=shared.at[source],
            dst_ref=shared.at[source],
            send_sem=share_send.at[0],
            recv_sem=share_recv.at[source],
            device_id=(place, source),
            device_id_type=MESH,
        )

    def score(g):
        p = ordered(g, odd, PIECES)
        width = factor.shape[0]
        for c in range(chunks):
            for k in range(1, tm_count):
                z_arrival(c, g, k).wait_recv()
        total = None
        for source in range(tm_count):
            cells = jnp.concatenate(
                [received[place_of(source, c, p)].reshape(part * block, LANES) for c in range(chunks)], axis=1
            )
            product = jnp.dot(
                cells, factor[source * slab : (source + 1) * slab, :], preferred_element_type=jnp.float32
            )
            total = product if total is None else total + product
        square = total * total
        folded = square[:, :LANES]
        for c in range(1, width // LANES):
            folded = folded + square[:, c * LANES : (c + 1) * LANES]
        for j in range(part):
            column = jnp.sum(folded[j * block : (j + 1) * block, :].T, axis=0, keepdims=True)
            shared[me, pl.ds(p * part + j, 1), :] = column / width

    slow_copy(0).start()
    fast_copy(0).start()
    for n in range(1, AHEAD):
        slow_copy(n).start()
    for c in range(chunks):
        own_copy(c).start()
    blocks_copy(0).start()
    factor_copy = pltpu.make_async_copy(factor_ref, factor, factor_sem)
    factor_copy.start()
    for c in range(chunks):
        near[c][3 * blocks_dev] = jnp.zeros((block, LANES), jnp.bfloat16)

    for c in range(chunks):
        own_copy(c).wait()
        fast_copy(c).wait()
        if c + 1 < chunks:
            fast_copy(c + 1).start()

        def stage(g, carry):
            n = c * PIECES + g
            p = ordered(g, odd, PIECES)

            @pl.when(n + 1 < steps_all)
            def _():
                blocks_copy(n + 1).start()

            arriving = slow_copy(n)
            arriving.wait_recv()
            arriving.wait_send()

            @pl.when(n + AHEAD < steps_all)
            def _():
                slow_copy(n + AHEAD).start()

            near[c][pl.ds(odd * (2 * blocks_dev) + p * piece_blocks, piece_blocks)] = land[n]
            blocks_copy(n).wait()
            slot = lax.rem(n, 2)

            def row(i, carry):
                base = (p * piece_blocks + i) * slots
                weights = jnp.concatenate([blocks_buf[slot, i, k] for k in range(slots)], axis=1)
                picked = jnp.concatenate(
                    [near[c][pos_ref[base + k]] for k in range(slots)], axis=0
                )
                spatial[c * PIECES + p, i] = jnp.dot(
                    weights, picked, preferred_element_type=jnp.float32
                ).astype(jnp.bfloat16)
                return carry

            lax.fori_loop(0, piece_blocks, row, 0, unroll=2)

            for k in range(1, tm_count):
                z_copy(c, g, k).start()
            received[place_of(me, c, p)] = spatial[c * PIECES + p, pl.ds(me * part, part)]

            if c + 1 == chunks:

                @pl.when(g >= LAG)
                def _():
                    score(g - LAG)

            return carry

        if c + 1 == chunks:
            factor_copy.wait()
        lax.fori_loop(0, PIECES, stage, 0)

    def last(g, carry):
        score(g)
        return carry

    lax.fori_loop(PIECES - LAG, PIECES, last, 0)
    for k in range(1, tm_count):
        share_copy(k).start()
    for c in range(chunks):

        def finish(g, carry):
            for k in range(1, tm_count):
                z_copy(c, g, k).wait_send()
            return carry

        lax.fori_loop(0, PIECES, finish, 0)
    for k in range(1, tm_count):
        share_arrival(k).wait_recv()

    def give(r, carry):
        b = me * (blocks_dev // tm_count) + r
        p, i = b // piece_blocks, lax.rem(b, piece_blocks)
        out_ref[pl.ds(r, 1), :] = shared[i // part, pl.ds(p * part + lax.rem(i, part), 1), :]
        return carry

    lax.fori_loop(0, blocks_dev // tm_count, give, 0)
    for k in range(1, tm_count):
        share_copy(k).wait_send()


def on_device(field, sp_blocks, sp_cols, sp_count, tm_factor):
    blocks_dev, slots, block, _ = sp_blocks.shape
    nodes, slab = field.shape
    space_count, tm_count = lax.axis_size("space"), lax.axis_size("tm")
    total_blocks = blocks_dev * space_count
    chunks = slab // LANES
    local = jnp.arange(blocks_dev, dtype=jnp.int32)[:, None]
    row_index = lax.axis_index("space") * blocks_dev + local
    position = local + jnp.mod(sp_cols - row_index + blocks_dev, total_blocks)
    alive = jnp.arange(slots, dtype=jnp.int32)[None, :] < sp_count[:, None]
    position = jnp.where(alive, position, 3 * blocks_dev).reshape(-1)

    piece_blocks = blocks_dev // PIECES
    part = piece_blocks // tm_count
    rows = nodes // tm_count
    steps_all = chunks * PIECES
    any_spec = pl.BlockSpec(memory_space=pl.ANY)
    dma = pltpu.SemaphoreType.DMA
    out = pl.pallas_call(
        functools.partial(kernel, (blocks_dev, slots, block, chunks, space_count, tm_count)),
        out_shape=jax.ShapeDtypeStruct((rows // LANES, LANES), jnp.float32),
        in_specs=[any_spec, any_spec, pl.BlockSpec(memory_space=pltpu.SMEM), any_spec],
        out_specs=pl.BlockSpec(memory_space=pltpu.VMEM),
        scratch_shapes=[pltpu.VMEM((3 * blocks_dev + 1, block, LANES), jnp.bfloat16) for _ in range(chunks)]
        + [
            pltpu.VMEM((steps_all, piece_blocks, block, LANES), jnp.bfloat16),
            pltpu.VMEM((2, piece_blocks, slots, block, block), jnp.bfloat16),
            pltpu.VMEM((steps_all, piece_blocks, block, LANES), jnp.bfloat16),
            pltpu.VMEM((tm_count * steps_all, part, block, LANES), jnp.bfloat16),
            pltpu.VMEM(tm_factor.shape, jnp.bfloat16),
            dma((chunks,)),
            dma((chunks,)),
            dma((chunks,)),
            dma((steps_all,)),
            dma((steps_all,)),
            dma((2,)),
            dma((steps_all * (tm_count - 1),)),
            dma((tm_count * steps_all,)),
            dma,
            pltpu.VMEM((tm_count, PIECES * part, LANES), jnp.float32),
            dma((tm_count - 1,)),
            dma((tm_count,)),
        ],
        compiler_params=pltpu.CompilerParams(
            collective_id=0, has_side_effects=True, vmem_limit_bytes=58 << 20
        ),
        cost_estimate=pl.CostEstimate(
            flops=2 * nodes * slab * (block * slots + tm_factor.shape[1]),
            bytes_accessed=2 * sp_blocks.size * chunks + 4 * field.size + 2 * tm_factor.size,
            transcendentals=0,
        ),
    )(field.reshape(blocks_dev, block, slab), sp_blocks, position, tm_factor)
    return out.reshape(rows)


def solution(mesh):
    in_specs = (P("space", "tm"), P("space", None, None, None), P("space", None), P("space"), P())
    out_specs = P(("space", "tm"))
    return jax.shard_map(
        on_device, mesh=mesh, in_specs=in_specs, out_specs=out_specs, check_vma=False
    )
```
